256 devices in a mesh: dp: 8 (over x, core), seq: 32 (over y, z).
Axes of the slice: x: 4, y: 4, z: 8, core: 2. Of those that a mesh axis runs over, the one named last changes fastest.
Arguments:
- layer_input: bfloat16 [8, 4096, 4096], P('dp', 'seq'), may hold values from -6 to 6
- queries: bfloat16 [8, 4096, 4096], P('dp', 'seq'), may hold values from -5 to 5
- rotated_key_states: bfloat16 [8, 4096, 1024], P('dp', 'seq'), may hold values from -5 to 5
- value_projection_weight: bfloat16 [4096, 1024], P('seq'), may hold values from -0.09375 to 0.09375
- out_grad: bfloat16 [8, 4096, 4096], P('dp', 'seq'), may hold values from -6 to 6
- key_blocks: int32 [8, 32, 8], P('dp'), may hold values from 0 to 31, as said below
- block_counts: int32 [8, 32], P('dp'), may hold values from 1 to 8, as said below
Outputs:
- attention_out: bfloat16 [8, 4096, 4096], P('dp', 'seq')
- query_grad: bfloat16 [8, 4096, 4096], P('dp', 'seq')
- key_state_gradient: bfloat16 [8, 4096, 1024], P('dp', 'seq')
- input_grad: bfloat16 [8, 4096, 4096], P('dp', 'seq')
- weight_grad: float32 [4096, 1024], P('seq')
The draws below stay inside these ranges and needn't reach their ends.
Inputs may be any that keep to these rules, and one draw needn't show every extreme that they name: `key_blocks`: in query block b the listed blocks lie at or before b: slot 0 is b itself, slot 1 is block 0 when b > 0, the first min(8, b + 1) slots are distinct, and any later slot repeats b. `block_counts`: at most b + 1 for query block b; the last block of every sequence has all 8 slots live.
All inputs are finite; a program needn't handle non-finite values.
Results may differ from the reference program's by a relative error of at most 0.019.
Values may be sent and summed in bfloat16 or wider, within the bound.
No kernel may reach another device: no remote copies, remote signals or barrier semaphores. Data moves between devices by JAX's collectives and lax.ppermute only.
A program may use at most 128 MiB of HBM per device.

```python
import jax
import jax.numpy as jnp
from jax import lax

MODEL_DIMENSION = 4096
QUERY_HEADS = 32
KEY_VALUE_HEADS = 8
HEAD_SIZE = 128
BLOCK = 128
SLOTS = 8
SEQUENCE_LENGTH = 4096
QB = 32
SEQUENCE_COUNT = 8


def draw_queries(key, part):
    key = jax.random.fold_in(key, 12)
    random_field = jnp.clip(jax.random.normal(key, (SEQUENCE_COUNT, SEQUENCE_LENGTH, QUERY_HEADS * HEAD_SIZE), jnp.float32), -5.0, 5.0)
    return random_field.astype(jnp.bfloat16)


def draw_rotated_key_states(key, part):
    key = jax.random.fold_in(key, 11)
    random_field = jnp.clip(jax.random.normal(key, (SEQUENCE_COUNT, SEQUENCE_LENGTH, KEY_VALUE_HEADS * HEAD_SIZE), jnp.float32), -5.0, 5.0)
    return random_field.astype(jnp.bfloat16)


def draw_key_blocks(key, part):
    key = jax.random.fold_in(key, 21)
    noise = jax.random.randint(key, (SEQUENCE_COUNT, QB, QB), 0, 65536)
    column = jnp.arange(QB, dtype=jnp.int32)[None, None, :]
    row_index = jnp.arange(QB, dtype=jnp.int32)[None, :, None]
    ranked = noise * QB + column
    ranked = jnp.where(column == row_index, 2 ** 30, jnp.where(column == 0, 2 ** 29, jnp.where(column < row_index, ranked, -1 - column)))
    chosen = lax.top_k(ranked, SLOTS)[1].astype(jnp.int32)
    return jnp.where(chosen > row_index, row_index, chosen).astype(jnp.int32)


def draw_block_counts(key, part):
    key = jax.random.fold_in(key, 22)
    drawn = jax.random.randint(key, (SEQUENCE_COUNT, QB), 1, SLOTS + 1)
    ceiling = jnp.arange(QB, dtype=jnp.int32)[None, :] + 1
    drawn = jnp.minimum(drawn, ceiling)
    return drawn.at[:, QB - 1].set(SLOTS).astype(jnp.int32)


def levels(stream_key, extent, cuts, smallest, top_value):
    gain = 1.0
    for axis_at, shards_of in cuts:
        draws = jax.random.uniform(jax.random.fold_in(jax.random.fold_in(stream_key, 6), axis_at), (shards_of,), jnp.float32, smallest / len(cuts), top_value / len(cuts))
        gain = gain * jnp.repeat(jnp.exp(draws), extent[axis_at] // shards_of).reshape((-1,) + (1,) * (len(extent) - 1 - axis_at))
    return gain


def bell_draw(stream_key, shape, deviation, most, shards=(), kind=jnp.bfloat16):
    loudness = levels(stream_key, shape, shards, -0.22, 0.18) if shards else 1.0
    result = jax.random.normal(stream_key, shape, jnp.float32) * deviation * loudness
    return jnp.minimum(jnp.maximum(result, -most), most).astype(kind)


def setup_inputs(seed: int = 0) -> dict:
    keys = jax.random.split(jax.random.key(seed), 8)
    layer_input = bell_draw(keys[0], (SEQUENCE_COUNT, SEQUENCE_LENGTH, MODEL_DIMENSION), 1.0, 6.0, ((0, 8), (1, 32)))
    queries = draw_queries(jax.random.fold_in(keys[7], 71), 0)
    rotated_key_states = draw_rotated_key_states(jax.random.fold_in(keys[7], 71), 0)
    value_projection_weight = bell_draw(keys[3], (MODEL_DIMENSION, KEY_VALUE_HEADS * HEAD_SIZE), MODEL_DIMENSION ** -0.5, 0.09375, ((0, 32),))
    out_grad = bell_draw(keys[4], (SEQUENCE_COUNT, SEQUENCE_LENGTH, QUERY_HEADS * HEAD_SIZE), 1.0, 6.0, ((0, 8), (1, 32)))
    key_blocks = draw_key_blocks(jax.random.fold_in(keys[7], 71), 0)
    block_counts = draw_block_counts(jax.random.fold_in(keys[7], 71), 0)
    return dict(layer_input=layer_input, queries=queries, rotated_key_states=rotated_key_states, value_projection_weight=value_projection_weight, out_grad=out_grad, key_blocks=key_blocks, block_counts=block_counts)


def head_pass(pieces):
    query_head, key_head, value_head, grad_head, slot_table, slot_live = pieces
    span = SLOTS * BLOCK
    score_scale = HEAD_SIZE ** -0.5
    query_tiles = query_head.reshape(QB, BLOCK, HEAD_SIZE)
    key_tiles = key_head.reshape(QB, BLOCK, HEAD_SIZE)
    value_tiles = value_head.reshape(QB, BLOCK, HEAD_SIZE)
    grad_tiles = grad_head.reshape(QB, BLOCK, HEAD_SIZE)
    slot_of = jnp.arange(span, dtype=jnp.int32) // BLOCK
    inside = jnp.arange(span, dtype=jnp.int32) % BLOCK
    causal = inside[None, :] <= jnp.arange(BLOCK, dtype=jnp.int32)[:, None]

    def step(carry, block):
        key_total, value_total = carry
        slot_rows = slot_table[block]
        key_rows = key_tiles[slot_rows].reshape(span, HEAD_SIZE)
        value_rows = value_tiles[slot_rows].reshape(span, HEAD_SIZE)
        query_rows = query_tiles[block]
        grad_rows = grad_tiles[block]
        is_live = slot_of < slot_live[block]
        is_diag = slot_rows[slot_of] == block
        allowed = is_live[None, :] & (jnp.logical_not(is_diag)[None, :] | causal)
        scores = jnp.dot(query_rows, key_rows.T, preferred_element_type=jnp.float32) * score_scale
        scores = jnp.where(allowed, scores, -1e30)
        largest = jnp.max(scores, axis=1, keepdims=True)
        exp_terms = jnp.where(allowed, jnp.exp(scores - largest), 0.0)
        weights = exp_terms / jnp.sum(exp_terms, axis=1, keepdims=True)
        rounded = weights.astype(jnp.bfloat16)
        output = jnp.dot(rounded, value_rows, preferred_element_type=jnp.float32).astype(jnp.bfloat16)
        row_delta = jnp.sum(grad_rows.astype(jnp.float32) * output.astype(jnp.float32), axis=1, keepdims=True)
        grad_probs = jnp.dot(grad_rows, value_rows.T, preferred_element_type=jnp.float32)
        grad_scores = (weights * (grad_probs - row_delta)).astype(jnp.bfloat16)
        grad_query = (jnp.dot(grad_scores, key_rows, preferred_element_type=jnp.float32) * score_scale).astype(jnp.bfloat16)
        key_terms = jnp.dot(grad_scores.T, query_rows, preferred_element_type=jnp.float32) * score_scale
        value_terms = jnp.dot(rounded.T, grad_rows, preferred_element_type=jnp.float32)
        key_total = key_total.at[slot_rows].add(key_terms.reshape(SLOTS, BLOCK, HEAD_SIZE))
        value_total = value_total.at[slot_rows].add(value_terms.reshape(SLOTS, BLOCK, HEAD_SIZE))
        return (key_total, value_total), (output, grad_query)

    zeros = jnp.zeros((QB, BLOCK, HEAD_SIZE), jnp.float32)
    (key_total, value_total), (outputs, query_grads) = lax.scan(step, (zeros, zeros), jnp.arange(QB, dtype=jnp.int32))
    return (outputs.reshape(SEQUENCE_LENGTH, HEAD_SIZE), query_grads.reshape(SEQUENCE_LENGTH, HEAD_SIZE),
            key_total.reshape(SEQUENCE_LENGTH, HEAD_SIZE).astype(jnp.bfloat16), value_total.reshape(SEQUENCE_LENGTH, HEAD_SIZE).astype(jnp.bfloat16))


def split_into_heads(stacked, head_total, repeat_by):
    moved = jnp.transpose(stacked.reshape(SEQUENCE_COUNT, SEQUENCE_LENGTH, head_total, HEAD_SIZE), (0, 2, 1, 3))
    return jnp.repeat(moved, repeat_by, axis=1).reshape(SEQUENCE_COUNT * head_total * repeat_by, SEQUENCE_LENGTH, HEAD_SIZE)


def merge_into_tokens(stacked, head_total):
    return jnp.transpose(stacked.reshape(SEQUENCE_COUNT, head_total, SEQUENCE_LENGTH, HEAD_SIZE), (0, 2, 1, 3)).reshape(SEQUENCE_COUNT, SEQUENCE_LENGTH, head_total * HEAD_SIZE)


def reference(layer_input, queries, rotated_key_states, value_projection_weight, out_grad, key_blocks, block_counts):
    heads_per_group = QUERY_HEADS // KEY_VALUE_HEADS
    flat_input = layer_input.reshape(SEQUENCE_COUNT * SEQUENCE_LENGTH, MODEL_DIMENSION)
    value_states = jnp.dot(flat_input, value_projection_weight, preferred_element_type=jnp.float32).astype(jnp.bfloat16)
    query_heads = split_into_heads(queries, QUERY_HEADS, 1)
    heads_of_keys = split_into_heads(rotated_key_states, KEY_VALUE_HEADS, heads_per_group)
    heads_of_values = split_into_heads(value_states, KEY_VALUE_HEADS, heads_per_group)
    grad_heads = split_into_heads(out_grad, QUERY_HEADS, 1)
    tables = jnp.repeat(key_blocks, QUERY_HEADS, axis=0)
    lives = jnp.repeat(block_counts, QUERY_HEADS, axis=0)
    outputs, query_grads, key_gradient_list, value_gradient_list = lax.map(
        head_pass, (query_heads, heads_of_keys, heads_of_values, grad_heads, tables, lives))
    attention_out = merge_into_tokens(outputs, QUERY_HEADS)
    query_grad = merge_into_tokens(query_grads, QUERY_HEADS)
    summed_key_gradient = jnp.sum(key_gradient_list.reshape(SEQUENCE_COUNT, KEY_VALUE_HEADS, heads_per_group, SEQUENCE_LENGTH, HEAD_SIZE).astype(jnp.float32), axis=2).astype(jnp.bfloat16)
    summed_value_gradient = jnp.sum(value_gradient_list.reshape(SEQUENCE_COUNT, KEY_VALUE_HEADS, heads_per_group, SEQUENCE_LENGTH, HEAD_SIZE).astype(jnp.float32), axis=2).astype(jnp.bfloat16)
    key_state_gradient = merge_into_tokens(summed_key_gradient, KEY_VALUE_HEADS)
    value_state_gradient = merge_into_tokens(summed_value_gradient, KEY_VALUE_HEADS).reshape(SEQUENCE_COUNT * SEQUENCE_LENGTH, KEY_VALUE_HEADS * HEAD_SIZE)
    input_grad = jnp.dot(value_state_gradient, value_projection_weight.T, preferred_element_type=jnp.float32).astype(jnp.bfloat16)
    weight_grad = jnp.dot(flat_input.T, value_state_gradient, preferred_element_type=jnp.float32)
    return (attention_out, query_grad, key_state_gradient, input_grad.reshape(SEQUENCE_COUNT, SEQUENCE_LENGTH, MODEL_DIMENSION), weight_grad)
```

```python
import functools

import jax
import jax.numpy as jnp
from jax import lax
from jax.experimental import pallas as pl
from jax.experimental.pallas import tpu as pltpu
from jax.sharding import PartitionSpec as P

HEAD = 128
BLOCK = 128
SLOTS = 8
NY = 4
NZ = 8
NX = 4
GROUP = 4
KV = 2
LOG2E = 1.4426950408889634
SCALE = HEAD**-0.5
BF16 = jnp.bfloat16
F32 = jnp.float32

ANY = pl.BlockSpec(memory_space=pl.ANY)
SMEM = pl.BlockSpec(memory_space=pltpu.SMEM)
VMEM = pl.BlockSpec(memory_space=pltpu.VMEM)


def dot(a, b, dims):
    return lax.dot_general(a, b, (dims, ((), ())), preferred_element_type=F32)


NN = ((1,), (0,))
NT = ((1,), (1,))
TN = ((0,), (0,))


def shift_y(a, s):
    perm = [(y * NZ + z, ((y + s) % NY) * NZ + z) for y in range(NY) for z in range(NZ)]
    return lax.ppermute(a, "seq", perm)


def shift_z(a, s):
    perm = [(y * NZ + z, y * NZ + (z + s) % NZ) for y in range(NY) for z in range(NZ)]
    return lax.ppermute(a, "seq", perm)


def shift_x(a, s):
    perm = [(2 * x + c, 2 * ((x + s) % NX) + c) for x in range(NX) for c in range(2)]
    return lax.ppermute(a, "dp", perm)


def swap_core(a):
    perm = [(2 * x + c, 2 * x + 1 - c) for x in range(NX) for c in range(2)]
    return lax.ppermute(a, "dp", perm)


def gather_z(own):
    half = own.shape[0] // 2
    up = [own]
    down = [own]
    for _ in range(3):
        up.append(shift_z(up[-1], 1))
        down.append(shift_z(down[-1], -1))
    far_a = shift_z(up[3][:half], 1)
    far_b = shift_z(down[3][half:], -1)
    return [own, up[1], up[2], up[3], far_a, far_b, down[3], down[2], down[1]]


def add(a, b):
    return (a.astype(F32) + b.astype(F32)).astype(BF16)


def reduce_z(parts):
    own, p1, p2, p3, far_a, far_b, m3, m2, m1 = parts
    half = own.shape[0] // 2
    down = shift_z(far_a, -1)
    up = shift_z(far_b, 1)
    down = jnp.concatenate([add(p3[:half], down), p3[half:]], 0)
    up = jnp.concatenate([m3[:half], add(m3[half:], up)], 0)
    down = shift_z(down, -1)
    up = shift_z(up, 1)
    down = shift_z(add(p2, down), -1)
    up = shift_z(add(m2, up), 1)
    down = shift_z(add(p1, down), -1)
    up = shift_z(add(m1, up), 1)
    return (own.astype(F32) + down.astype(F32) + up.astype(F32)).astype(BF16)


def split_kernel(count, place, *refs):
    ins, outs = refs[:count], refs[count:]
    y = place[0]
    for i in range(count):
        width = ins[i].shape[1] // NY
        for s in range(NY):
            columns = pl.ds(pl.multiple_of(lax.rem(y + s, NY) * width, 128), width)
            outs[NY * i + s][...] = ins[i][:, columns]


def split_columns(place, *arrays):
    n = len(arrays)
    outs = pl.pallas_call(
        functools.partial(split_kernel, n),
        out_shape=[
            jax.ShapeDtypeStruct((a.shape[0], a.shape[1] // NY), a.dtype)
            for a in arrays
            for _ in range(NY)
        ],
        in_specs=[SMEM] + [VMEM] * n,
        out_specs=[VMEM] * (NY * n),
        compiler_params=pltpu.CompilerParams(vmem_limit_bytes=32 * 2**20),
        name="split_columns",
    )(place, *arrays)
    return [outs[NY * i : NY * i + NY] for i in range(n)]


def join_kernel(place, *refs):
    ins, out = refs[:NY], refs[NY]
    y = place[0]
    width = ins[0].shape[1]
    for s in range(NY):
        columns = pl.ds(pl.multiple_of(lax.rem(y + s, NY) * width, 128), width)
        out[:, columns] = ins[s][...]


def join_columns(place, pieces):
    rows, width = pieces[0].shape
    return pl.pallas_call(
        join_kernel,
        out_shape=jax.ShapeDtypeStruct((rows, NY * width), pieces[0].dtype),
        in_specs=[SMEM] + [VMEM] * NY,
        out_specs=VMEM,
        compiler_params=pltpu.CompilerParams(vmem_limit_bytes=32 * 2**20),
        name="join_columns",
    )(place, *pieces)


def send_back(pieces):
    return [pieces[0]] + [shift_y(pieces[s], -s) for s in range(1, NY)]


def project_kernel(place, *refs):
    xs, ws = refs[:4], refs[4:13]
    outs, w_out = refs[13:17], refs[17]
    xbuf, wbuf, sems = refs[18:]
    z = place[1]
    copies = [pltpu.make_async_copy(xs[s], xbuf.at[pl.ds(s * BLOCK, BLOCK)], sems.at[s]) for s in range(4)]
    row = lambda r: lax.rem(z - r + NZ, NZ) * BLOCK
    starts = [row(0), row(1), row(2), row(3), row(4), row(4) + BLOCK // 2, row(5), row(6), row(7)]
    for i in range(9):
        rows = ws[i].shape[0]
        copies.append(
            pltpu.make_async_copy(
                ws[i], wbuf.at[pl.ds(pl.multiple_of(starts[i], BLOCK // 2), rows)], sems.at[4 + i]
            )
        )
    for c in copies:
        c.start()
    for c in copies:
        c.wait()
    out_copy = pltpu.make_async_copy(wbuf, w_out, sems.at[0])
    out_copy.start()
    for t in range(NY):
        group = wbuf[:, t * 256 : (t + 1) * 256]
        for s in range(NY):
            got = dot(xbuf[s * BLOCK : (s + 1) * BLOCK, :], group, NN).astype(BF16)
            outs[t][(s - t) % NY] = got
    out_copy.wait()


def project(place, xs, ws):
    return pl.pallas_call(
        project_kernel,
        out_shape=[jax.ShapeDtypeStruct((NY, BLOCK, 256), BF16)] * NY
        + [jax.ShapeDtypeStruct((1024, 1024), BF16)],
        in_specs=[SMEM] + [ANY] * 13,
        out_specs=[VMEM] * NY + [ANY],
        scratch_shapes=[
            pltpu.VMEM((512, 1024), BF16),
            pltpu.VMEM((1024, 1024), BF16),
            pltpu.SemaphoreType.DMA((13,)),
        ],
        compiler_params=pltpu.CompilerParams(vmem_limit_bytes=32 * 2**20),
        name="project",
    )(place, *xs, *ws)


def chunk_starts(sems, pieces, buf, first):
    at = [0, 4, 8, 12, 16, 18, 20, 24, 28]
    return [
        pltpu.make_async_copy(pieces[i], buf.at[pl.ds(at[i], pieces[i].shape[0])], sems.at[first + i])
        for i in range(9)
    ]


def load_all(qs, dos, ks, vs, qbuf, dobuf, kbuf, vbuf, sems):
    copies = chunk_starts(sems, ks, kbuf, 0) + chunk_starts(sems, vs, vbuf, 9)
    for s in range(NY):
        copies.append(pltpu.make_async_copy(qs[s], qbuf.at[s], sems.at[18 + s]))
        copies.append(pltpu.make_async_copy(dos[s], dobuf.at[s], sems.at[22 + s]))
    for c in copies:
        c.start()
    for c in copies:
        c.wait()


def unit_places(place, table, counts, s):
    y, z = place[0], place[1]
    b = lax.rem(y - s + NY, NY) * NZ + z
    places = []
    for i in range(SLOTS):
        idx = table[b, i]
        places.append(lax.rem(z - lax.rem(idx, NZ) + NZ, NZ) * NY + lax.rem(y - idx // NZ + NY, NY))
    return counts[b], places


def stack_heads(buf, s, g):
    base = pl.multiple_of(g * (GROUP * HEAD), GROUP * HEAD)
    rows = buf[s, :, pl.ds(base, GROUP * HEAD)]
    return jnp.concatenate([rows[:, h * HEAD : (h + 1) * HEAD] for h in range(GROUP)], 0)


def masked_scores(kg, q4, j, chunks, count):
    scores = dot(kg[j * 256 : (j + 1) * 256, :], q4, NT)
    key = lax.broadcasted_iota(jnp.int32, (128, 512), 0)
    query = lax.rem(lax.broadcasted_iota(jnp.int32, (128, 512), 1), BLOCK)
    top, bottom = scores[:128], scores[128:]
    if j == 0:
        top = jnp.where(key <= query, top, -1e30)
    if j == chunks - 1:
        bottom = jnp.where(count > 2 * j + 1, bottom, -1e30)
    return jnp.concatenate([top, bottom], 0)


def forward_kernel(place, table, counts, *refs):
    qs, dos, ks, vs = refs[:4], refs[4:8], refs[8:17], refs[17:26]
    os, dvs, stats = refs[26:30], refs[30:39], refs[39]
    qbuf, dobuf, kbuf, vbuf, kg, vg, sbuf, obuf, acc, sems = refs[40:]
    load_all(qs, dos, ks, vs, qbuf, dobuf, kbuf, vbuf, sems)
    acc[...] = jnp.zeros_like(acc)

    def unit(u, _):
        s, g = u // KV, lax.rem(u, KV)
        count, places = unit_places(place, table, counts, s)
        lanes = pl.ds(pl.multiple_of(g * HEAD, HEAD), HEAD)

        def body(chunks):
            for i in range(2 * chunks):
                kg[i * BLOCK : (i + 1) * BLOCK, :] = kbuf[places[i], :, lanes]
                vg[i * BLOCK : (i + 1) * BLOCK, :] = vbuf[places[i], :, lanes]
            q4 = stack_heads(qbuf, s, g)
            do4 = stack_heads(dobuf, s, g)
            largest = None
            for j in range(chunks):
                scores = masked_scores(kg, q4, j, chunks, count)
                sbuf[j * 256 : (j + 1) * 256, :] = scores
                top = jnp.max(scores, axis=0, keepdims=True)
                largest = top if largest is None else jnp.maximum(largest, top)
            total = None
            for j in range(chunks):
                e = jnp.exp2((sbuf[j * 256 : (j + 1) * 256, :] - largest) * (SCALE * LOG2E))
                sbuf[j * 256 : (j + 1) * 256, :] = e
                part = jnp.sum(e, axis=0, keepdims=True)
                total = part if total is None else total + part
            inverse = 1.0 / total
            out_t = None
            for j in range(chunks):
                p = (sbuf[j * 256 : (j + 1) * 256, :] * inverse).astype(BF16)
                part = dot(vg[j * 256 : (j + 1) * 256, :], p, TN)
                out_t = part if out_t is None else out_t + part
                grad = dot(p, do4, NN)
                for i in range(2):
                    at = places[2 * j + i]
                    acc[at, :, lanes] = acc[at, :, lanes] + grad[i * BLOCK : (i + 1) * BLOCK, :]
            stats[u, 0:1, :] = largest * (SCALE * LOG2E) + jnp.log2(total)
            low_t = out_t.astype(BF16).astype(F32)
            do_t = jnp.transpose(do4.astype(F32))
            stats[u, 1:2, :] = jnp.sum(low_t * do_t, axis=0, keepdims=True)
            for h in range(GROUP):
                columns = pl.ds(pl.multiple_of(g * (GROUP * HEAD), GROUP * HEAD) + h * HEAD, HEAD)
                obuf[s, :, columns] = jnp.transpose(low_t[:, h * HEAD : (h + 1) * HEAD]).astype(BF16)

        pairs = (count + 1) // 2
        for chunks in range(1, SLOTS // 2 + 1):
            pl.when(pairs == chunks)(functools.partial(body, chunks))
        return 0

    lax.fori_loop(0, NY * KV, unit, 0)
    out_copies = [pltpu.make_async_copy(obuf.at[s], os[s], sems.at[s]) for s in range(NY)]
    for c in out_copies:
        c.start()
    at = [0, 4, 8, 12, 16, 18, 20, 24, 28]
    for i in range(9):
        n = dvs[i].shape[0]
        dvs[i][...] = acc[at[i] : at[i] + n].astype(BF16)
    for c in out_copies:
        c.wait()


PIECES = [NY, NY, NY, NY, NY // 2, NY // 2, NY, NY, NY]


def attention_forward(place, table, counts, qs, dos, ks, vs):
    outs = pl.pallas_call(
        forward_kernel,
        out_shape=[jax.ShapeDtypeStruct((BLOCK, 1024), BF16)] * NY
        + [jax.ShapeDtypeStruct((n, BLOCK, KV * HEAD), BF16) for n in PIECES]
        + [jax.ShapeDtypeStruct((NY * KV, 2, GROUP * BLOCK), F32)],
        in_specs=[SMEM] * 3 + [ANY] * 26,
        out_specs=[ANY] * NY + [VMEM] * 10,
        scratch_shapes=[
            pltpu.VMEM((NY, BLOCK, 1024), BF16),
            pltpu.VMEM((NY, BLOCK, 1024), BF16),
            pltpu.VMEM((32, BLOCK, KV * HEAD), BF16),
            pltpu.VMEM((32, BLOCK, KV * HEAD), BF16),
            pltpu.VMEM((SLOTS * BLOCK, HEAD), BF16),
            pltpu.VMEM((SLOTS * BLOCK, HEAD), BF16),
            pltpu.VMEM((SLOTS * BLOCK, GROUP * BLOCK), F32),
            pltpu.VMEM((NY, BLOCK, 1024), BF16),
            pltpu.VMEM((32, BLOCK, KV * HEAD), F32),
            pltpu.SemaphoreType.DMA((26,)),
        ],
        compiler_params=pltpu.CompilerParams(vmem_limit_bytes=48 * 2**20),
        cost_estimate=pl.CostEstimate(flops=8 * 10**9, bytes_accessed=10 * 2**20, transcendentals=4 * 2**20),
        name="attention_forward",
    )(place, table, counts, *qs, *dos, *ks, *vs)
    return outs[:4], outs[4:13], outs[13]


def backward_kernel(place, table, counts, stats, *refs):
    qs, dos, ks, vs = refs[:4], refs[4:8], refs[8:17], refs[17:26]
    dqs, dks = refs[26:30], refs[30:39]
    qbuf, dobuf, kbuf, vbuf, kg, vg, dqbuf, acc, sems = refs[39:]
    load_all(qs, dos, ks, vs, qbuf, dobuf, kbuf, vbuf, sems)
    acc[...] = jnp.zeros_like(acc)

    def unit(u, _):
        s, g = u // KV, lax.rem(u, KV)
        count, places = unit_places(place, table, counts, s)
        lanes = pl.ds(pl.multiple_of(g * HEAD, HEAD), HEAD)

        def body(chunks):
            for i in range(2 * chunks):
                kg[i * BLOCK : (i + 1) * BLOCK, :] = kbuf[places[i], :, lanes]
                vg[i * BLOCK : (i + 1) * BLOCK, :] = vbuf[places[i], :, lanes]
            q4 = stack_heads(qbuf, s, g)
            do4 = stack_heads(dobuf, s, g)
            lse = stats[u, 0:1, :]
            delta = stats[u, 1:2, :]
            dq_t = None
            for j in range(chunks):
                scores = masked_scores(kg, q4, j, chunks, count)
                p = jnp.exp2(scores * (SCALE * LOG2E) - lse)
                dp = dot(vg[j * 256 : (j + 1) * 256, :], do4, NT)
                ds = (p * (dp - delta)).astype(BF16)
                part = dot(kg[j * 256 : (j + 1) * 256, :], ds, TN)
                dq_t = part if dq_t is None else dq_t + part
                grad = dot(ds, q4, NN)
                for i in range(2):
                    at = places[2 * j + i]
                    acc[at, :, lanes] = acc[at, :, lanes] + grad[i * BLOCK : (i + 1) * BLOCK, :]
            dq_t = dq_t * SCALE
            for h in range(GROUP):
                columns = pl.ds(pl.multiple_of(g * (GROUP * HEAD), GROUP * HEAD) + h * HEAD, HEAD)
                dqbuf[s, :, columns] = jnp.transpose(dq_t[:, h * HEAD : (h + 1) * HEAD]).astype(BF16)

        pairs = (count + 1) // 2
        for chunks in range(1, SLOTS // 2 + 1):
            pl.when(pairs == chunks)(functools.partial(body, chunks))
        return 0

    lax.fori_loop(0, NY * KV, unit, 0)
    out_copies = [pltpu.make_async_copy(dqbuf.at[s], dqs[s], sems.at[s]) for s in range(NY)]
    for c in out_copies:
        c.start()
    at = [0, 4, 8, 12, 16, 18, 20, 24, 28]
    for i in range(9):
        n = dks[i].shape[0]
        dks[i][...] = (acc[at[i] : at[i] + n] * SCALE).astype(BF16)
    for c in out_copies:
        c.wait()


def attention_backward(place, table, counts, stats, qs, dos, ks, vs):
    outs = pl.pallas_call(
        backward_kernel,
        out_shape=[jax.ShapeDtypeStruct((BLOCK, 1024), BF16)] * NY
        + [jax.ShapeDtypeStruct((n, BLOCK, KV * HEAD), BF16) for n in PIECES],
        in_specs=[SMEM] * 3 + [VMEM] + [ANY] * 26,
        out_specs=[ANY] * NY + [VMEM] * 9,
        scratch_shapes=[
            pltpu.VMEM((NY, BLOCK, 1024), BF16),
            pltpu.VMEM((NY, BLOCK, 1024), BF16),
            pltpu.VMEM((32, BLOCK, KV * HEAD), BF16),
            pltpu.VMEM((32, BLOCK, KV * HEAD), BF16),
            pltpu.VMEM((SLOTS * BLOCK, HEAD), BF16),
            pltpu.VMEM((SLOTS * BLOCK, HEAD), BF16),
            pltpu.VMEM((NY, BLOCK, 1024), BF16),
            pltpu.VMEM((32, BLOCK, KV * HEAD), F32),
            pltpu.SemaphoreType.DMA((26,)),
        ],
        compiler_params=pltpu.CompilerParams(vmem_limit_bytes=48 * 2**20),
        cost_estimate=pl.CostEstimate(flops=10 * 10**9, bytes_accessed=10 * 2**20, transcendentals=4 * 2**20),
        name="attention_backward",
    )(place, table, counts, stats, *qs, *dos, *ks, *vs)
    return outs[:4], outs[4:13]


def per_device(layer_input, queries, keys, weight, out_grad, key_blocks, block_counts):
    seq = lax.axis_index("seq")
    dp = lax.axis_index("dp")
    y, z = seq // NZ, seq % NZ
    x, core = dp // 2, dp % 2
    place = jnp.stack([y, z]).astype(jnp.int32)
    table, counts = key_blocks[0], block_counts[0]

    weight_rel = jnp.concatenate(
        [lax.dynamic_slice_in_dim(weight, ((y - t) % NY) * 256, 256, 1) for t in range(NY)], 1
    )
    w_pieces = gather_z(weight_rel)
    x_split, k_split = split_columns(place, layer_input[0], keys[0])
    q_split, do_split = split_columns(place, queries[0], out_grad[0])
    spread = lambda p: [p[0]] + [shift_y(p[s], s) for s in range(1, NY)]
    ks = gather_z(jnp.stack(spread(k_split)))
    xs = spread(x_split)
    *v_parts, w_full = project(place, xs, w_pieces)
    v_got = [v_parts[0]] + [shift_y(v_parts[t], -t) for t in range(1, NY)]
    v_own = sum(v.astype(F32) for v in v_got).astype(BF16)
    vs = gather_z(v_own)
    qs = spread(q_split)
    dos = spread(do_split)

    o_pieces, dv_pieces, stats = attention_forward(place, table, counts, qs, dos, ks, vs)
    dv_own = reduce_z(dv_pieces)
    attention_out = join_columns(place, send_back(o_pieces))
    dq_pieces, dk_pieces = attention_backward(place, table, counts, stats, qs, dos, ks, vs)

    dv_all = [dv_own] + [shift_y(dv_own, t) for t in range(1, NY)]
    dv_full = jnp.concatenate([jnp.roll(dv_all[t], t, 0).reshape(NY * BLOCK, 256) for t in range(NY)], 1)
    x_full = jnp.concatenate(xs, 0)
    dw = dot(x_full, dv_full, TN).astype(BF16)
    dx = dot(dv_full, w_full, NT).astype(BF16)
    mine = lax.dynamic_slice_in_dim(dw, core * 512, 512, 1)
    other = lax.dynamic_slice_in_dim(dw, (1 - core) * 512, 512, 1)
    dw = add(mine, swap_core(other))
    quarters = [lax.dynamic_slice_in_dim(dw, ((x + s) % NX) * 128, 128, 1) for s in range(NX)]
    dw = (
        quarters[0].astype(F32) + sum(shift_x(quarters[s], s).astype(F32) for s in range(1, NX))
    ).astype(BF16)
    rows = [lax.dynamic_slice_in_dim(dw, ((z + r) % NZ) * 128, 128, 0) for r in range(NZ)]
    dw = rows[0].astype(F32) + sum(shift_z(rows[r], r).astype(F32) for r in range(1, NZ))
    dw = dw.astype(BF16)
    around = jnp.concatenate([dw] + [shift_x(dw, s) for s in range(1, NX)], 1)
    around = jnp.concatenate([lax.dynamic_slice_in_dim(around, ((x - i) % NX) * 128, 128, 1) for i in range(NX)], 1)
    swapped = swap_core(around)
    both = jnp.concatenate([jnp.where(core == 0, around, swapped), jnp.where(core == 0, swapped, around)], 1)
    weight_grad = jnp.concatenate(
        [lax.dynamic_slice_in_dim(both, ((y - i) % NY) * 256, 256, 1) for i in range(NY)], 1
    ).astype(F32)

    dx_pieces = [dx[s * BLOCK : (s + 1) * BLOCK] for s in range(NY)]
    input_grad = join_columns(place, send_back(dx_pieces))
    query_grad = join_columns(place, send_back(dq_pieces))
    dk_own = reduce_z(dk_pieces)
    key_grad = join_columns(place, send_back([dk_own[s] for s in range(NY)]))
    return attention_out[None], query_grad[None], key_grad[None], input_grad[None], weight_grad


def solution(mesh):
    placed = (
        P("dp", "seq", None),
        P("dp", "seq", None),
        P("dp", "seq", None),
        P("seq", None),
        P("dp", "seq", None),
        P("dp", None, None),
        P("dp", None),
    )
    return jax.shard_map(
        per_device,
        mesh=mesh,
        in_specs=placed,
        out_specs=(
            P("dp", "seq", None),
            P("dp", "seq", None),
            P("dp", "seq", None),
            P("dp", "seq", None),
            P("seq", None),
        ),
        check_vma=False,
    )
```

```python
import functools

import jax
import jax.numpy as jnp
from jax import lax
from jax.experimental import pallas as pl
from jax.experimental.pallas import tpu as pltpu
from jax.sharding import PartitionSpec as P

HEAD = 128
BLOCK = 128
SLOTS = 8
NY = 4
NZ = 8
NX = 4
GROUP = 4
KV = 2
LOG2E = 1.4426950408889634
SCALE = HEAD**-0.5
BF16 = jnp.bfloat16
F32 = jnp.float32

ANY = pl.BlockSpec(memory_space=pl.ANY)
SMEM = pl.BlockSpec(memory_space=pltpu.SMEM)
VMEM = pl.BlockSpec(memory_space=pltpu.VMEM)


def dot(a, b, dims):
    return lax.dot_general(a, b, (dims, ((), ())), preferred_element_type=F32)


NN = ((1,), (0,))
NT = ((1,), (1,))
TN = ((0,), (0,))


def shift_y(a, s):
    perm = [(y * NZ + z, ((y + s) % NY) * NZ + z) for y in range(NY) for z in range(NZ)]
    return lax.ppermute(a, "seq", perm)


def shift_z(a, s):
    perm = [(y * NZ + z, y * NZ + (z + s) % NZ) for y in range(NY) for z in range(NZ)]
    return lax.ppermute(a, "seq", perm)


def shift_x(a, s):
    perm = [(2 * x + c, 2 * ((x + s) % NX) + c) for x in range(NX) for c in range(2)]
    return lax.ppermute(a, "dp", perm)


def swap_core(a):
    perm = [(2 * x + c, 2 * x + 1 - c) for x in range(NX) for c in range(2)]
    return lax.ppermute(a, "dp", perm)


ALONG_Z = [[y * NZ + z for z in range(NZ)] for y in range(NY)]


def after(a, *others):
    return lax.optimization_barrier((a, others))[0]


def split_kernel(count, place, *refs):
    ins, outs = refs[:count], refs[count:]
    y = place[0]
    for i in range(count):
        width = ins[i].shape[1] // NY
        for s in range(NY):
            columns = pl.ds(pl.multiple_of(lax.rem(y + s, NY) * width, 128), width)
            outs[NY * i + s][...] = ins[i][:, columns]


def split_columns(place, *arrays):
    n = len(arrays)
    outs = pl.pallas_call(
        functools.partial(split_kernel, n),
        out_shape=[
            jax.ShapeDtypeStruct((a.shape[0], a.shape[1] // NY), a.dtype)
            for a in arrays
            for _ in range(NY)
        ],
        in_specs=[SMEM] + [VMEM] * n,
        out_specs=[VMEM] * (NY * n),
        compiler_params=pltpu.CompilerParams(vmem_limit_bytes=32 * 2**20),
        name="split_columns",
    )(place, *arrays)
    return [outs[NY * i : NY * i + NY] for i in range(n)]


def join_kernel(place, *refs):
    ins, out = refs[:NY], refs[NY]
    y = place[0]
    width = ins[0].shape[1]
    for s in range(NY):
        columns = pl.ds(pl.multiple_of(lax.rem(y + s, NY) * width, 128), width)
        out[:, columns] = ins[s][...]


def join_columns(place, pieces):
    rows, width = pieces[0].shape
    return pl.pallas_call(
        join_kernel,
        out_shape=jax.ShapeDtypeStruct((rows, NY * width), pieces[0].dtype),
        in_specs=[SMEM] + [VMEM] * NY,
        out_specs=VMEM,
        compiler_params=pltpu.CompilerParams(vmem_limit_bytes=32 * 2**20),
        name="join_columns",
    )(place, *pieces)


def send_back(pieces):
    return [pieces[0]] + [shift_y(pieces[s], -s) for s in range(1, NY)]


FETCH = ((0, 4), (1, -3), (-1, 3), (2, -2))


def fetch_weight(own):
    perm = []
    for x in range(NX):
        for c in range(2):
            for y in range(NY):
                for z in range(NZ):
                    device = (2 * x + c) * NY * NZ + y * NZ
                    perm.append((device + (z - FETCH[x][c]) % NZ, device + z))
    first = lax.ppermute(own, ("dp", "seq"), perm)
    mine = [first] + [shift_x(first, s) for s in range(1, NX)]
    return mine + [swap_core(w) for w in mine]


def project_kernel(place, *refs):
    xs, ws = refs[:4], refs[4:12]
    outs, w_out = refs[12:16], refs[16]
    xbuf, wbuf, sems = refs[17:]
    z, x, core = place[1], place[2], place[3]
    copies = [pltpu.make_async_copy(xs[s], xbuf.at[pl.ds(s * BLOCK, BLOCK)], sems.at[s]) for s in range(4)]
    for k in range(2):
        for s in range(NX):
            distance = place[4 + 2 * lax.rem(x - s + NX, NX) + lax.rem(core + k, 2)]
            rows = pl.ds(pl.multiple_of(lax.rem(z - distance + NZ, NZ) * BLOCK, BLOCK), BLOCK)
            i = NX * k + s
            copies.append(pltpu.make_async_copy(ws[i], wbuf.at[rows], sems.at[4 + i]))
    for c in copies:
        c.start()
    for c in copies:
        c.wait()
    out_copy = pltpu.make_async_copy(wbuf, w_out, sems.at[0])
    out_copy.start()
    for t in range(NY):
        group = wbuf[:, t * 256 : (t + 1) * 256]
        for s in range(NY):
            got = dot(xbuf[s * BLOCK : (s + 1) * BLOCK, :], group, NN).astype(BF16)
            outs[t][(s - t) % NY] = got
    out_copy.wait()


def project(place, xs, ws):
    return pl.pallas_call(
        project_kernel,
        out_shape=[jax.ShapeDtypeStruct((NY, BLOCK, 256), BF16)] * NY
        + [jax.ShapeDtypeStruct((1024, 1024), BF16)],
        in_specs=[SMEM] + [ANY] * 12,
        out_specs=[VMEM] * NY + [ANY],
        scratch_shapes=[
            pltpu.VMEM((512, 1024), BF16),
            pltpu.VMEM((1024, 1024), BF16),
            pltpu.SemaphoreType.DMA((12,)),
        ],
        compiler_params=pltpu.CompilerParams(vmem_limit_bytes=60 * 2**20),
        name="project",
    )(place, *xs, *ws)


def load_all(qs, dos, ks, vs, qbuf, dobuf, kbuf, vbuf, sems):
    copies = [
        pltpu.make_async_copy(ks, kbuf, sems.at[0]),
        pltpu.make_async_copy(vs, vbuf, sems.at[1]),
    ]
    for s in range(NY):
        copies.append(pltpu.make_async_copy(qs[s], qbuf.at[s], sems.at[2 + s]))
        copies.append(pltpu.make_async_copy(dos[s], dobuf.at[s], sems.at[6 + s]))
    for c in copies:
        c.start()
    return copies


def unit_places(place, table, counts, s):
    y = place[0]
    b = lax.rem(y - s + NY, NY) * NZ + place[1]
    places = []
    for i in range(SLOTS):
        idx = table[b, i]
        places.append(lax.rem(idx, NZ) * NY + lax.rem(y - idx // NZ + NY, NY))
    return counts[b], places


def stack_heads(buf, s, g):
    base = pl.multiple_of(g * (GROUP * HEAD), GROUP * HEAD)
    rows = buf[s, :, pl.ds(base, GROUP * HEAD)]
    return jnp.concatenate([rows[:, h * HEAD : (h + 1) * HEAD] for h in range(GROUP)], 0)


def masked_scores(kg, q4, j, chunks, count):
    scores = dot(kg[j * 256 : (j + 1) * 256, :], q4, NT)
    key = lax.broadcasted_iota(jnp.int32, (128, 512), 0)
    query = lax.rem(lax.broadcasted_iota(jnp.int32, (128, 512), 1), BLOCK)
    top, bottom = scores[:128], scores[128:]
    if j == 0:
        top = jnp.where(key <= query, top, -1e30)
    if j == chunks - 1:
        bottom = jnp.where(count > 2 * j + 1, bottom, -1e30)
    return jnp.concatenate([top, bottom], 0)


def attention_kernel(place, table, counts, *refs):
    qs, dos, ks, vs = refs[:4], refs[4:8], refs[8], refs[9]
    os, dqs, dv, dk = refs[10:14], refs[14:18], refs[18], refs[19]
    qbuf, dobuf, kbuf, vbuf, kg, vg, sbuf, obuf, dqbuf, vacc, kacc, sems, vsems, ksems = refs[20:]
    copies = load_all(qs, dos, ks, vs, qbuf, dobuf, kbuf, vbuf, sems)
    vacc[...] = jnp.zeros_like(vacc)
    kacc[...] = jnp.zeros_like(kacc)
    for c in copies:
        c.wait()

    def unit(u, _):
        s, g = u // KV, lax.rem(u, KV)
        count, places = unit_places(place, table, counts, s)
        lanes = pl.ds(pl.multiple_of(g * HEAD, HEAD), HEAD)

        def body(chunks):
            for i in range(2 * chunks):
                kg[i * BLOCK : (i + 1) * BLOCK, :] = kbuf[places[i], :, lanes]
                vg[i * BLOCK : (i + 1) * BLOCK, :] = vbuf[places[i], :, lanes]
            q4 = stack_heads(qbuf, s, g)
            do4 = stack_heads(dobuf, s, g)
            do_t = jnp.transpose(do4.astype(F32))

            def add_to(acc, j, grad):
                for i in range(2):
                    at = places[2 * j + i]
                    acc[at, :, lanes] = acc[at, :, lanes] + grad[i * BLOCK : (i + 1) * BLOCK, :]

            def store_heads(buf, value_t):
                for h in range(GROUP):
                    columns = pl.ds(pl.multiple_of(g * (GROUP * HEAD), GROUP * HEAD) + h * HEAD, HEAD)
                    buf[s, :, columns] = jnp.transpose(value_t[:, h * HEAD : (h + 1) * HEAD]).astype(BF16)

            largest = None
            for j in range(chunks):
                scores = masked_scores(kg, q4, j, chunks, count)
                sbuf[j * 256 : (j + 1) * 256, :] = scores
                top = jnp.max(scores, axis=0, keepdims=True)
                largest = top if largest is None else jnp.maximum(largest, top)
            total = None
            for j in range(chunks):
                e = jnp.exp2((sbuf[j * 256 : (j + 1) * 256, :] - largest) * (SCALE * LOG2E))
                sbuf[j * 256 : (j + 1) * 256, :] = e
                part = jnp.sum(e, axis=0, keepdims=True)
                total = part if total is None else total + part
            inverse = 1.0 / total
            out_t = None
            for j in range(chunks):
                low = (sbuf[j * 256 : (j + 1) * 256, :] * inverse).astype(BF16)
                part = dot(vg[j * 256 : (j + 1) * 256, :], low, TN)
                out_t = part if out_t is None else out_t + part
                add_to(vacc, j, dot(low, do4, NN))
            low_t = out_t.astype(BF16).astype(F32)
            delta = jnp.sum(low_t * do_t, axis=0, keepdims=True)
            store_heads(obuf, low_t)
            dq_t = None
            for j in range(chunks):
                dp = dot(vg[j * 256 : (j + 1) * 256, :], do4, NT)
                ds = (sbuf[j * 256 : (j + 1) * 256, :] * ((dp - delta) * inverse)).astype(BF16)
                part = dot(kg[j * 256 : (j + 1) * 256, :], ds, TN)
                dq_t = part if dq_t is None else dq_t + part
                add_to(kacc, j, dot(ds, q4, NN))
            store_heads(dqbuf, dq_t * SCALE)

        pairs = (count + 1) // 2
        for chunks in range(1, SLOTS // 2 + 1):
            pl.when(pairs == chunks)(functools.partial(body, chunks))
        return 0

    lax.fori_loop(0, NY * KV, unit, 0)
    out_copies = [pltpu.make_async_copy(obuf.at[s], os[s], sems.at[s]) for s in range(NY)]
    out_copies += [pltpu.make_async_copy(dqbuf.at[s], dqs[s], sems.at[NY + s]) for s in range(NY)]
    for c in out_copies:
        c.start()
    for i in range(NZ):
        rows = pl.ds(i * NY, NY)
        vbuf[rows] = vacc[rows].astype(BF16)
        copy = pltpu.make_async_copy(vbuf.at[rows], dv.at[rows], vsems.at[i])
        copy.start()
        out_copies.append(copy)
    for i in range(NZ):
        rows = pl.ds(i * NY, NY)
        kbuf[rows] = (kacc[rows] * SCALE).astype(BF16)
        copy = pltpu.make_async_copy(kbuf.at[rows], dk.at[rows], ksems.at[i])
        copy.start()
        out_copies.append(copy)
    for c in out_copies:
        c.wait()


def attention(place, table, counts, qs, dos, ks, vs):
    outs = pl.pallas_call(
        attention_kernel,
        out_shape=[jax.ShapeDtypeStruct((BLOCK, 1024), BF16)] * (2 * NY)
        + [jax.ShapeDtypeStruct((32, BLOCK, KV * HEAD), BF16)] * 2,
        in_specs=[SMEM] * 3 + [ANY] * 10,
        out_specs=[ANY] * (2 * NY + 2),
        scratch_shapes=[
            pltpu.VMEM((NY, BLOCK, 1024), BF16),
            pltpu.VMEM((NY, BLOCK, 1024), BF16),
            pltpu.VMEM((32, BLOCK, KV * HEAD), BF16),
            pltpu.VMEM((32, BLOCK, KV * HEAD), BF16),
            pltpu.VMEM((SLOTS * BLOCK, HEAD), BF16),
            pltpu.VMEM((SLOTS * BLOCK, HEAD), BF16),
            pltpu.VMEM((SLOTS * BLOCK, GROUP * BLOCK), F32),
            pltpu.VMEM((NY, BLOCK, 1024), BF16),
            pltpu.VMEM((NY, BLOCK, 1024), BF16),
            pltpu.VMEM((32, BLOCK, KV * HEAD), F32),
            pltpu.VMEM((32, BLOCK, KV * HEAD), F32),
            pltpu.SemaphoreType.DMA((10,)),
            pltpu.SemaphoreType.DMA((NZ,)),
            pltpu.SemaphoreType.DMA((NZ,)),
        ],
        compiler_params=pltpu.CompilerParams(vmem_limit_bytes=60 * 2**20),
        cost_estimate=pl.CostEstimate(flops=16 * 10**9, bytes_accessed=14 * 2**20, transcendentals=4 * 2**20),
        name="attention",
    )(place, table, counts, *qs, *dos, ks, vs)
    return outs[:4], outs[4:8], outs[8], outs[9]


def quarters_kernel(place, mine, got, *outs):
    x = place[2]
    for s in range(NX):
        columns = pl.ds(pl.multiple_of(lax.rem(x + s, NX) * 128, 128), 128)
        outs[s][...] = (mine[:, columns].astype(F32) + got[:, columns].astype(F32)).astype(BF16)


def add_quarters(place, mine, got):
    return pl.pallas_call(
        quarters_kernel,
        out_shape=[jax.ShapeDtypeStruct((1024, 128), BF16)] * NX,
        in_specs=[SMEM, VMEM, VMEM],
        out_specs=[VMEM] * NX,
        compiler_params=pltpu.CompilerParams(vmem_limit_bytes=32 * 2**20),
        name="add_quarters",
    )(place, mine, got)


def rows_kernel(*refs):
    ins, out = refs[:NX], refs[NX]
    out[...] = sum(i[...].astype(F32) for i in ins).astype(BF16)


def add_rows(pieces):
    return pl.pallas_call(
        rows_kernel,
        out_shape=jax.ShapeDtypeStruct((1024, 128), BF16),
        in_specs=[VMEM] * NX,
        out_specs=VMEM,
        name="add_rows",
    )(*pieces)


def weight_kernel(place, *refs):
    ins, out = refs[: 2 * NX], refs[2 * NX]
    y, x, core = place[0], place[2], place[3]
    for s in range(NX):
        for k in range(2):
            xs = lax.rem(x - s + NX, NX)
            cs = lax.rem(core + k, 2)
            group = lax.rem(y - 2 * cs - xs // 2 + NY, NY)
            columns = pl.ds(pl.multiple_of(group * 256 + lax.rem(xs, 2) * 128, 128), 128)
            out[:, columns] = ins[2 * s + k][...].astype(F32)


def place_weight(place, pieces):
    return pl.pallas_call(
        weight_kernel,
        out_shape=jax.ShapeDtypeStruct((128, 1024), F32),
        in_specs=[SMEM] + [VMEM] * (2 * NX),
        out_specs=VMEM,
        name="place_weight",
    )(place, *pieces)


def per_device(layer_input, queries, keys, weight, out_grad, key_blocks, block_counts):
    seq = lax.axis_index("seq")
    dp = lax.axis_index("dp")
    y, z = seq // NZ, seq % NZ
    x, core = dp // 2, dp % 2
    fetch = jnp.asarray([d for pair in FETCH for d in pair], jnp.int32)
    place = jnp.concatenate([jnp.stack([y, z, x, core]).astype(jnp.int32), fetch])
    table, counts = key_blocks[0], block_counts[0]
    spread = lambda p: [p[0]] + [shift_y(p[s], s) for s in range(1, NY)]

    x_split, k_split = split_columns(place, layer_input[0], keys[0])
    xs = spread(x_split)
    weight_rel = jnp.concatenate(
        [lax.dynamic_slice_in_dim(weight, ((y - t) % NY) * 256, 256, 1) for t in range(NY)], 1
    )
    along_z = dict(tiled=True, axis_index_groups=ALONG_Z)
    ws = fetch_weight(weight_rel)
    k_own = jnp.stack(spread([after(k, ws[0]) for k in k_split]))
    ks = lax.all_gather(k_own, "seq", axis=0, **along_z)
    q_split, do_split = split_columns(place, queries[0], out_grad[0])
    *v_parts, w_full = project(place, xs, ws)
    v_got = [v_parts[0]] + [shift_y(v_parts[t], -t) for t in range(1, NY)]
    v_own = sum(v.astype(F32) for v in v_got).astype(BF16)
    vs = lax.all_gather(v_own, "seq", axis=0, **along_z)
    qs = spread([after(q, v_own) for q in q_split])
    dos = spread([after(d, *qs) for d in do_split])

    o_pieces, dq_pieces, dv, dk = attention(place, table, counts, qs, dos, ks, vs)
    o_back = send_back(o_pieces)
    attention_out = join_columns(place, o_back)
    dq_pieces = [after(d, *o_back) for d in dq_pieces]
    dq_back = send_back(dq_pieces)
    query_grad = join_columns(place, dq_back)
    dv_own = lax.psum_scatter(dv, "seq", scatter_dimension=0, **along_z)
    dv_own = after(dv_own, query_grad)
    dk_own = lax.psum_scatter(after(dk, dv_own), "seq", scatter_dimension=0, **along_z)

    dv_all = [dv_own] + [shift_y(dv_own, t) for t in range(1, NY)]
    dv_full = jnp.concatenate([jnp.roll(dv_all[t], t, 0).reshape(NY * BLOCK, 256) for t in range(NY)], 1)
    x_full = jnp.concatenate(xs, 0)
    half = lambda c: dot(x_full, lax.dynamic_slice_in_dim(dv_full, c * 512, 512, 1), TN).astype(BF16)
    got = swap_core(half(1 - core))
    dx = dot(dv_full, w_full, NT).astype(BF16)
    dx_back = send_back([dx[s * BLOCK : (s + 1) * BLOCK] for s in range(NY)])
    quarters = add_quarters(place, half(core), got)
    quarters = [quarters[0]] + [shift_x(quarters[s], s) for s in range(1, NX)]
    input_grad = join_columns(place, dx_back)
    quarters[0] = after(quarters[0], attention_out, input_grad)
    dw_rows = add_rows(quarters)
    dw = lax.all_to_all(dw_rows, "seq", 0, 0, **along_z).reshape(NZ, 128, 128)
    dw = jnp.sum(dw.astype(F32), 0).astype(BF16)
    key_grad = join_columns(place, send_back([dk_own[s] for s in range(NY)]))
    dw = after(dw, key_grad)
    around = jnp.stack([dw] + [shift_x(dw, s) for s in range(1, NX)])
    swapped = swap_core(around)
    pieces = [p for s in range(NX) for p in (around[s], swapped[s])]
    weight_grad = place_weight(place, pieces)
    return attention_out[None], query_grad[None], key_grad[None], input_grad[None], weight_grad


def solution(mesh):
    placed = (
        P("dp", "seq", None),
        P("dp", "seq", None),
        P("dp", "seq", None),
        P("seq", None),
        P("dp", "seq", None),
        P("dp", None, None),
        P("dp", None),
    )
    return jax.shard_map(
        per_device,
        mesh=mesh,
        in_specs=placed,
        out_specs=(
            P("dp", "seq", None),
            P("dp", "seq", None),
            P("dp", "seq", None),
            P("dp", "seq", None),
            P("seq", None),
        ),
        check_vma=False,
    )
```

```python
import functools

import jax
import jax.numpy as jnp
from jax import lax
from jax.experimental import pallas as pl
from jax.experimental.pallas import tpu as pltpu
from jax.sharding import PartitionSpec as P

HEAD = 128
BLOCK = 128
SLOTS = 8
NY = 4
NZ = 8
NX = 4
GROUP = 4
KV = 2
LOG2E = 1.4426950408889634
SCALE = HEAD**-0.5
BF16 = jnp.bfloat16
F32 = jnp.float32

ANY = pl.BlockSpec(memory_space=pl.ANY)
SMEM = pl.BlockSpec(memory_space=pltpu.SMEM)
VMEM = pl.BlockSpec(memory_space=pltpu.VMEM)


def dot(a, b, dims):
    return lax.dot_general(a, b, (dims, ((), ())), preferred_element_type=F32)


NN = ((1,), (0,))
NT = ((1,), (1,))
TN = ((0,), (0,))


def shift_y(a, s):
    perm = [(y * NZ + z, ((y + s) % NY) * NZ + z) for y in range(NY) for z in range(NZ)]
    return lax.ppermute(a, "seq", perm)


def shift_z(a, s):
    perm = [(y * NZ + z, y * NZ + (z + s) % NZ) for y in range(NY) for z in range(NZ)]
    return lax.ppermute(a, "seq", perm)


def shift_x(a, s):
    perm = [(2 * x + c, 2 * ((x + s) % NX) + c) for x in range(NX) for c in range(2)]
    return lax.ppermute(a, "dp", perm)


def swap_core(a):
    perm = [(2 * x + c, 2 * x + 1 - c) for x in range(NX) for c in range(2)]
    return lax.ppermute(a, "dp", perm)


ALONG_Z = [[y * NZ + z for z in range(NZ)] for y in range(NY)]


def after(a, *others):
    return lax.optimization_barrier((a, others))[0]


def split_kernel(count, place, *refs):
    ins, outs = refs[:count], refs[count:]
    y = place[0]
    for i in range(count):
        width = ins[i].shape[1] // NY
        for s in range(NY):
            columns = pl.ds(pl.multiple_of(lax.rem(y + s, NY) * width, 128), width)
            outs[NY * i + s][...] = ins[i][:, columns]


def split_columns(place, *arrays):
    n = len(arrays)
    outs = pl.pallas_call(
        functools.partial(split_kernel, n),
        out_shape=[
            jax.ShapeDtypeStruct((a.shape[0], a.shape[1] // NY), a.dtype)
            for a in arrays
            for _ in range(NY)
        ],
        in_specs=[SMEM] + [VMEM] * n,
        out_specs=[VMEM] * (NY * n),
        compiler_params=pltpu.CompilerParams(vmem_limit_bytes=32 * 2**20),
        name="split_columns",
    )(place, *arrays)
    return [outs[NY * i : NY * i + NY] for i in range(n)]


def join_kernel(place, *refs):
    ins, out = refs[:NY], refs[NY]
    y = place[0]
    width = ins[0].shape[1]
    for s in range(NY):
        columns = pl.ds(pl.multiple_of(lax.rem(y + s, NY) * width, 128), width)
        out[:, columns] = ins[s][...]


def join_columns(place, pieces):
    rows, width = pieces[0].shape
    return pl.pallas_call(
        join_kernel,
        out_shape=jax.ShapeDtypeStruct((rows, NY * width), pieces[0].dtype),
        in_specs=[SMEM] + [VMEM] * NY,
        out_specs=VMEM,
        compiler_params=pltpu.CompilerParams(vmem_limit_bytes=32 * 2**20),
        name="join_columns",
    )(place, *pieces)


def send_back(pieces):
    return [pieces[0]] + [shift_y(pieces[s], -s) for s in range(1, NY)]


FETCH = ((0, 4), (1, -3), (-1, 3), (2, -2))


def fetch_weight(own):
    perm = []
    for x in range(NX):
        for c in range(2):
            for y in range(NY):
                for z in range(NZ):
                    device = (2 * x + c) * NY * NZ + y * NZ
                    perm.append((device + (z - FETCH[x][c]) % NZ, device + z))
    first = lax.ppermute(own, ("dp", "seq"), perm)
    mine = [first] + [shift_x(first, s) for s in range(1, NX)]
    return mine + [swap_core(w) for w in mine]


def project_kernel(place, *refs):
    xs, ws = refs[:4], refs[4:12]
    outs, w_out = refs[12:16], refs[16]
    xbuf, wbuf, sems = refs[17:]
    z, x, core = place[1], place[2], place[3]
    copies = [pltpu.make_async_copy(xs[s], xbuf.at[pl.ds(s * BLOCK, BLOCK)], sems.at[s]) for s in range(4)]
    for k in range(2):
        for s in range(NX):
            distance = place[4 + 2 * lax.rem(x - s + NX, NX) + lax.rem(core + k, 2)]
            rows = pl.ds(pl.multiple_of(lax.rem(z - distance + NZ, NZ) * BLOCK, BLOCK), BLOCK)
            i = NX * k + s
            copies.append(pltpu.make_async_copy(ws[i], wbuf.at[rows], sems.at[4 + i]))
    for c in copies:
        c.start()
    for c in copies:
        c.wait()
    out_copy = pltpu.make_async_copy(wbuf, w_out, sems.at[0])
    out_copy.start()
    for t in range(NY):
        group = wbuf[:, t * 256 : (t + 1) * 256]
        for s in range(NY):
            got = dot(xbuf[s * BLOCK : (s + 1) * BLOCK, :], group, NN).astype(BF16)
            outs[t][(s - t) % NY] = got
    out_copy.wait()


def project(place, xs, ws):
    return pl.pallas_call(
        project_kernel,
        out_shape=[jax.ShapeDtypeStruct((NY, BLOCK, 256), BF16)] * NY
        + [jax.ShapeDtypeStruct((1024, 1024), BF16)],
        in_specs=[SMEM] + [ANY] * 12,
        out_specs=[VMEM] * NY + [ANY],
        scratch_shapes=[
            pltpu.VMEM((512, 1024), BF16),
            pltpu.VMEM((1024, 1024), BF16),
            pltpu.SemaphoreType.DMA((12,)),
        ],
        compiler_params=pltpu.CompilerParams(vmem_limit_bytes=60 * 2**20),
        name="project",
    )(place, *xs, *ws)


def load_all(qs, dos, ks, vs, qbuf, dobuf, kbuf, vbuf, sems):
    copies = [
        pltpu.make_async_copy(ks, kbuf, sems.at[0]),
        pltpu.make_async_copy(vs, vbuf, sems.at[1]),
    ]
    for s in range(NY):
        copies.append(pltpu.make_async_copy(qs[s], qbuf.at[s], sems.at[2 + s]))
        copies.append(pltpu.make_async_copy(dos[s], dobuf.at[s], sems.at[6 + s]))
    for c in copies:
        c.start()
    return copies


def unit_places(place, table, counts, s):
    y = place[0]
    b = lax.rem(y - s + NY, NY) * NZ + place[1]
    places = []
    for i in range(SLOTS):
        idx = table[b, i]
        places.append(lax.rem(idx, NZ) * NY + lax.rem(y - idx // NZ + NY, NY))
    return counts[b], places


def stack_heads(buf, s, g):
    base = pl.multiple_of(g * (GROUP * HEAD), GROUP * HEAD)
    rows = buf[s, :, pl.ds(base, GROUP * HEAD)]
    return jnp.concatenate([rows[:, h * HEAD : (h + 1) * HEAD] for h in range(GROUP)], 0)


def masked_scores(kg, q4, j, chunks, count):
    scores = dot(kg[j * 256 : (j + 1) * 256, :], q4, NT)
    key = lax.broadcasted_iota(jnp.int32, (128, 512), 0)
    query = lax.rem(lax.broadcasted_iota(jnp.int32, (128, 512), 1), BLOCK)
    top, bottom = scores[:128], scores[128:]
    if j == 0:
        top = jnp.where(key <= query, top, -1e30)
    if j == chunks - 1:
        bottom = jnp.where(count > 2 * j + 1, bottom, -1e30)
    return jnp.concatenate([top, bottom], 0)


def attention_kernel(place, table, counts, *refs):
    qs, dos, ks, vs = refs[:4], refs[4:8], refs[8], refs[9]
    os, dqs, dv, dk = refs[10:14], refs[14:18], refs[18], refs[19]
    qbuf, dobuf, kbuf, vbuf, kg, vg, sbuf, obuf, dqbuf, vacc, kacc, sems, vsems, ksems = refs[20:]
    copies = load_all(qs, dos, ks, vs, qbuf, dobuf, kbuf, vbuf, sems)
    vacc[...] = jnp.zeros_like(vacc)
    kacc[...] = jnp.zeros_like(kacc)
    for c in copies:
        c.wait()

    def unit(u, _):
        s, g = u // KV, lax.rem(u, KV)
        count, places = unit_places(place, table, counts, s)
        lanes = pl.ds(pl.multiple_of(g * HEAD, HEAD), HEAD)

        def body(chunks):
            for i in range(2 * chunks):
                kg[i * BLOCK : (i + 1) * BLOCK, :] = kbuf[places[i], :, lanes]
                vg[i * BLOCK : (i + 1) * BLOCK, :] = vbuf[places[i], :, lanes]
            q4 = stack_heads(qbuf, s, g)
            do4 = stack_heads(dobuf, s, g)
            do_t = jnp.transpose(do4.astype(F32))

            def add_to(acc, j, grad):
                for i in range(2):
                    at = places[2 * j + i]
                    acc[at, :, lanes] = acc[at, :, lanes] + grad[i * BLOCK : (i + 1) * BLOCK, :]

            def store_heads(buf, value_t):
                for h in range(GROUP):
                    columns = pl.ds(pl.multiple_of(g * (GROUP * HEAD), GROUP * HEAD) + h * HEAD, HEAD)
                    buf[s, :, columns] = jnp.transpose(value_t[:, h * HEAD : (h + 1) * HEAD]).astype(BF16)

            largest = None
            for j in range(chunks):
                scores = masked_scores(kg, q4, j, chunks, count)
                sbuf[j * 256 : (j + 1) * 256, :] = scores
                top = jnp.max(scores, axis=0, keepdims=True)
                largest = top if largest is None else jnp.maximum(largest, top)
            total = None
            for j in range(chunks):
                e = jnp.exp2((sbuf[j * 256 : (j + 1) * 256, :] - largest) * (SCALE * LOG2E))
                sbuf[j * 256 : (j + 1) * 256, :] = e
                part = jnp.sum(e, axis=0, keepdims=True)
                total = part if total is None else total + part
            inverse = 1.0 / total
            out_t = None
            for j in range(chunks):
                low = (sbuf[j * 256 : (j + 1) * 256, :] * inverse).astype(BF16)
                part = dot(vg[j * 256 : (j + 1) * 256, :], low, TN)
                out_t = part if out_t is None else out_t + part
                add_to(vacc, j, dot(low, do4, NN))
            low_t = out_t.astype(BF16).astype(F32)
            delta = jnp.sum(low_t * do_t, axis=0, keepdims=True)
            store_heads(obuf, low_t)
            dq_t = None
            for j in range(chunks):
                dp = dot(vg[j * 256 : (j + 1) * 256, :], do4, NT)
                ds = (sbuf[j * 256 : (j + 1) * 256, :] * ((dp - delta) * inverse)).astype(BF16)
                part = dot(kg[j * 256 : (j + 1) * 256, :], ds, TN)
                dq_t = part if dq_t is None else dq_t + part
                add_to(kacc, j, dot(ds, q4, NN))
            store_heads(dqbuf, dq_t * SCALE)

        pairs = (count + 1) // 2
        for chunks in range(1, SLOTS // 2 + 1):
            pl.when(pairs == chunks)(functools.partial(body, chunks))
        return 0

    lax.fori_loop(0, NY * KV, unit, 0)
    out_copies = [pltpu.make_async_copy(obuf.at[s], os[s], sems.at[s]) for s in range(NY)]
    out_copies += [pltpu.make_async_copy(dqbuf.at[s], dqs[s], sems.at[NY + s]) for s in range(NY)]
    for c in out_copies:
        c.start()
    for i in range(NZ):
        rows = pl.ds(i * NY, NY)
        vbuf[rows] = vacc[rows].astype(BF16)
        copy = pltpu.make_async_copy(vbuf.at[rows], dv.at[rows], vsems.at[i])
        copy.start()
        out_copies.append(copy)
    for i in range(NZ):
        rows = pl.ds(i * NY, NY)
        kbuf[rows] = (kacc[rows] * SCALE).astype(BF16)
        copy = pltpu.make_async_copy(kbuf.at[rows], dk.at[rows], ksems.at[i])
        copy.start()
        out_copies.append(copy)
    for c in out_copies:
        c.wait()


def attention(place, table, counts, qs, dos, ks, vs):
    outs = pl.pallas_call(
        attention_kernel,
        out_shape=[jax.ShapeDtypeStruct((BLOCK, 1024), BF16)] * (2 * NY)
        + [jax.ShapeDtypeStruct((32, BLOCK, KV * HEAD), BF16)] * 2,
        in_specs=[SMEM] * 3 + [ANY] * 10,
        out_specs=[ANY] * (2 * NY + 2),
        scratch_shapes=[
            pltpu.VMEM((NY, BLOCK, 1024), BF16),
            pltpu.VMEM((NY, BLOCK, 1024), BF16),
            pltpu.VMEM((32, BLOCK, KV * HEAD), BF16),
            pltpu.VMEM((32, BLOCK, KV * HEAD), BF16),
            pltpu.VMEM((SLOTS * BLOCK, HEAD), BF16),
            pltpu.VMEM((SLOTS * BLOCK, HEAD), BF16),
            pltpu.VMEM((SLOTS * BLOCK, GROUP * BLOCK), F32),
            pltpu.VMEM((NY, BLOCK, 1024), BF16),
            pltpu.VMEM((NY, BLOCK, 1024), BF16),
            pltpu.VMEM((32, BLOCK, KV * HEAD), F32),
            pltpu.VMEM((32, BLOCK, KV * HEAD), F32),
            pltpu.SemaphoreType.DMA((10,)),
            pltpu.SemaphoreType.DMA((NZ,)),
            pltpu.SemaphoreType.DMA((NZ,)),
        ],
        compiler_params=pltpu.CompilerParams(vmem_limit_bytes=60 * 2**20),
        cost_estimate=pl.CostEstimate(flops=16 * 10**9, bytes_accessed=14 * 2**20, transcendentals=4 * 2**20),
        name="attention",
    )(place, table, counts, *qs, *dos, ks, vs)
    return outs[:4], outs[4:8], outs[8], outs[9]


def quarters_kernel(place, mine, got, *outs):
    x = place[2]
    for s in range(NX):
        columns = pl.ds(pl.multiple_of(lax.rem(x + s, NX) * 128, 128), 128)
        outs[s][...] = (mine[:, columns].astype(F32) + got[:, columns].astype(F32)).astype(BF16)


def add_quarters(place, mine, got):
    return pl.pallas_call(
        quarters_kernel,
        out_shape=[jax.ShapeDtypeStruct((1024, 128), BF16)] * NX,
        in_specs=[SMEM, VMEM, VMEM],
        out_specs=[VMEM] * NX,
        compiler_params=pltpu.CompilerParams(vmem_limit_bytes=32 * 2**20),
        name="add_quarters",
    )(place, mine, got)


def rows_kernel(*refs):
    ins, out = refs[:NX], refs[NX]
    out[...] = sum(i[...].astype(F32) for i in ins).astype(BF16)


def add_rows(pieces):
    return pl.pallas_call(
        rows_kernel,
        out_shape=jax.ShapeDtypeStruct((1024, 128), BF16),
        in_specs=[VMEM] * NX,
        out_specs=VMEM,
        name="add_rows",
    )(*pieces)


def weight_kernel(place, *refs):
    ins, out = refs[: 2 * NX], refs[2 * NX]
    y, x, core = place[0], place[2], place[3]
    for s in range(NX):
        for k in range(2):
            xs = lax.rem(x - s + NX, NX)
            cs = lax.rem(core + k, 2)
            group = lax.rem(y - 2 * cs - xs // 2 + NY, NY)
            columns = pl.ds(pl.multiple_of(group * 256 + lax.rem(xs, 2) * 128, 128), 128)
            out[:, columns] = ins[2 * s + k][...].astype(F32)


def place_weight(place, pieces):
    return pl.pallas_call(
        weight_kernel,
        out_shape=jax.ShapeDtypeStruct((128, 1024), F32),
        in_specs=[SMEM] + [VMEM] * (2 * NX),
        out_specs=VMEM,
        name="place_weight",
    )(place, *pieces)


def per_device(layer_input, queries, keys, weight, out_grad, key_blocks, block_counts):
    seq = lax.axis_index("seq")
    dp = lax.axis_index("dp")
    y, z = seq // NZ, seq % NZ
    x, core = dp // 2, dp % 2
    fetch = jnp.asarray([d for pair in FETCH for d in pair], jnp.int32)
    place = jnp.concatenate([jnp.stack([y, z, x, core]).astype(jnp.int32), fetch])
    table, counts = key_blocks[0], block_counts[0]
    spread = lambda p: [p[0]] + [shift_y(p[s], s) for s in range(1, NY)]

    x_split, k_split = split_columns(place, layer_input[0], keys[0])
    xs = spread(x_split)
    weight_rel = jnp.concatenate(
        [lax.dynamic_slice_in_dim(weight, ((y - t) % NY) * 256, 256, 1) for t in range(NY)], 1
    )
    along_z = dict(tiled=True, axis_index_groups=ALONG_Z)
    ws = fetch_weight(weight_rel)
    k_own = after(jnp.stack(spread(k_split)), ws[1], ws[3])
    ks = lax.all_gather(k_own, "seq", axis=0, **along_z)
    q_split, do_split = split_columns(place, queries[0], out_grad[0])
    *v_parts, w_full = project(place, xs, ws)
    v_got = [v_parts[0]] + [shift_y(v_parts[t], -t) for t in range(1, NY)]
    v_own = sum(v.astype(F32) for v in v_got).astype(BF16)
    vs = lax.all_gather(v_own, "seq", axis=0, **along_z)
    qs = spread([after(q, v_own) for q in q_split])
    dos = spread([after(d, *qs) for d in do_split])

    o_pieces, dq_pieces, dv, dk = attention(place, table, counts, qs, dos, ks, vs)
    o_back = send_back(o_pieces)
    attention_out = join_columns(place, o_back)
    dq_pieces = [after(d, *o_back) for d in dq_pieces]
    dq_back = send_back(dq_pieces)
    query_grad = join_columns(place, dq_back)
    dv_own = lax.psum_scatter(dv, "seq", scatter_dimension=0, **along_z)
    dv_own = after(dv_own, query_grad)
    dk_own = lax.psum_scatter(after(dk, dv_own), "seq", scatter_dimension=0, **along_z)

    dv_all = [dv_own] + [shift_y(dv_own, t) for t in range(1, NY)]
    dv_full = jnp.concatenate([jnp.roll(dv_all[t], t, 0).reshape(NY * BLOCK, 256) for t in range(NY)], 1)
    x_full = jnp.concatenate(xs, 0)
    half = lambda c: dot(x_full, lax.dynamic_slice_in_dim(dv_full, c * 512, 512, 1), TN).astype(BF16)
    got = swap_core(half(1 - core))
    dx = dot(dv_full, w_full, NT).astype(BF16)
    dx_back = send_back([dx[s * BLOCK : (s + 1) * BLOCK] for s in range(NY)])
    quarters = add_quarters(place, half(core), got)
    quarters = [quarters[0]] + [shift_x(quarters[s], s) for s in range(1, NX)]
    input_grad = join_columns(place, dx_back)
    quarters[0] = after(quarters[0], attention_out, input_grad)
    dw_rows = add_rows(quarters)
    dw = lax.all_to_all(dw_rows, "seq", 0, 0, **along_z).reshape(NZ, 128, 128)
    dw = jnp.sum(dw.astype(F32), 0).astype(BF16)
    key_grad = join_columns(place, send_back([dk_own[s] for s in range(NY)]))
    dw = after(dw, key_grad)
    around = jnp.stack([dw] + [shift_x(dw, s) for s in range(1, NX)])
    swapped = swap_core(around)
    pieces = [p for s in range(NX) for p in (around[s], swapped[s])]
    weight_grad = place_weight(place, pieces)
    return attention_out[None], query_grad[None], key_grad[None], input_grad[None], weight_grad


def solution(mesh):
    placed = (
        P("dp", "seq", None),
        P("dp", "seq", None),
        P("dp", "seq", None),
        P("seq", None),
        P("dp", "seq", None),
        P("dp", None, None),
        P("dp", None),
    )
    return jax.shard_map(
        per_device,
        mesh=mesh,
        in_specs=placed,
        out_specs=(
            P("dp", "seq", None),
            P("dp", "seq", None),
            P("dp", "seq", None),
            P("dp", "seq", None),
            P("seq", None),
        ),
        check_vma=False,
    )
```
